32 devices in a mesh: gz: 8 (over y, x, core), gy: 4 (over z).
Axes of the slice: x: 2, y: 2, z: 4, core: 2. Of those that a mesh axis runs over, the one named last changes fastest.
Arguments:
- potential: float32 [24, 512, 2048], P('gz', 'gy'), may hold values from -3 to 301
- external: float32 [24, 512, 2048], P('gz', 'gy'), may hold values from -4 to 4
Outputs:
- dual_field: float32 [24, 512, 2048], P('gz', 'gy')
- density_log: float32 [24, 512, 2048], P('gz', 'gy')
The draws below stay inside these ranges and needn't reach their ends.
All inputs are finite; a program needn't handle non-finite values.
Results may differ from the reference program's by a relative error of at most 0.0001.
Values sent between devices are 32-bit elements; how exact they have to be, the bound alone decides.
No kernel may reach another device: no remote copies, remote signals or barrier semaphores. Data moves between devices by JAX's collectives and lax.ppermute only.
A program may use at most 128 MiB of HBM per device.

```python
import jax
import jax.numpy as jnp
from jax import lax

NX = 2048
CY = 128
RADIUS = 128
NY = 512
NZ = 24
N_GY = 4


def draw_potential(key, part):
    field_shape = (NZ, NY, NX)
    exponent_tail = jnp.minimum(jax.random.exponential(key, field_shape, jnp.float32), 18.0)
    rough_part = 3.0 * exponent_tail - 3.0
    return rough_part


def levels(stream_key, shape, cuts, low, top_value):
    factor_of = 1.0
    for axis_at, parts in cuts:
        steps = jax.random.uniform(jax.random.fold_in(jax.random.fold_in(stream_key, 6), axis_at), (parts,), jnp.float32, low / len(cuts), top_value / len(cuts))
        factor_of = factor_of * jnp.repeat(jnp.exp(steps), shape[axis_at] // parts).reshape((-1,) + (1,) * (len(shape) - 1 - axis_at))
    return factor_of


def noise(key, extent, width, limit, cuts=(), held_as=jnp.bfloat16):
    level = levels(key, extent, cuts, -0.22, 0.18) if cuts else 1.0
    values = jax.random.normal(key, extent, jnp.float32) * width * level
    return jnp.minimum(jnp.maximum(values, -limit), limit).astype(held_as)


def setup_inputs(seed: int = 0) -> dict:
    arg_keys = jax.random.split(jax.random.key(seed), 3)
    potential = draw_potential(jax.random.fold_in(arg_keys[2], 71), 0)
    external = noise(arg_keys[1], (NZ, NY, NX), 1.0, 4.0, ((0, 8), (1, 4)), jnp.float32)
    return {"potential": potential, "external": external}


HIGHEST = lax.Precision.HIGHEST


def log_kernel(row_count, col_count, offset, radius):
    in_index = lax.broadcasted_iota(jnp.int32, (row_count, col_count), 0)
    out_index = lax.broadcasted_iota(jnp.int32, (row_count, col_count), 1)
    apart = in_index - offset - out_index
    distance = apart.astype(jnp.float32)
    inside = jnp.abs(apart) <= radius
    return jnp.where(inside, jnp.exp(-2.0 * distance * distance / float(radius * radius)), 0.0)


def along_last(source, radius):
    leading = source.shape[:-1]
    length = source.shape[-1]
    block_size = 2 * radius
    block_count = length // block_size
    border = jnp.full(leading + (radius,), -jnp.inf, jnp.float32)
    padded = jnp.concatenate([border, source, border], axis=-1)
    pieces = padded.reshape(leading + (block_count + 1, block_size))
    window = jnp.concatenate([pieces[..., :-1, :], pieces[..., 1:, :]], axis=-1)
    highest_value = jnp.max(window, axis=-1, keepdims=True)
    weights = jnp.exp(window - highest_value)
    kernel_table = log_kernel(2 * block_size, block_size, radius, radius)
    summed = jnp.einsum("...w,wo->...o", weights, kernel_table, precision=HIGHEST)
    return (jnp.log(summed) + highest_value).reshape(leading + (length,))


def along_middle(extended, own_rows, radius):
    highest_value = jnp.max(extended, axis=1, keepdims=True)
    weights = jnp.exp(extended - highest_value)
    kernel_table = log_kernel(own_rows + 2 * radius, own_rows, radius, radius)
    summed = jnp.einsum("zwx,wo->zox", weights, kernel_table, precision=HIGHEST)
    return jnp.log(summed) + highest_value


def along_first(source, radius):
    length = source.shape[0]
    highest_value = jnp.max(source, axis=0, keepdims=True)
    weights = jnp.exp(source - highest_value)
    kernel_table = log_kernel(length, length, 0, radius)
    summed = jnp.einsum("wyx,wo->oyx", weights, kernel_table, precision=HIGHEST)
    return jnp.log(summed) + highest_value


def proximal(logs, outer_field):
    shifted = logs - 0.5 * outer_field
    softer = jnp.maximum(shifted, 0.0) + jnp.log1p(jnp.exp(-jnp.abs(shifted)))
    log_level = jnp.log1p(softer)
    for newton_step in range(2):
        exp_level = jnp.exp(log_level)
        log_level = log_level - (log_level + exp_level - shifted) / (1.0 + exp_level)
    return log_level - logs, log_level


def reference(potential, external):
    depth = RADIUS

    def plane_pass(plane):
        along_x = along_last(plane, depth)
        border = jnp.full((depth, NX), -jnp.inf, jnp.float32)
        padded = jnp.concatenate([border, along_x, border], axis=0)
        results = []
        for block_index in range(N_GY):
            window = lax.slice_in_dim(padded, block_index * CY, block_index * CY + CY + 2 * depth, axis=0)
            results.append(along_middle(window[None], CY, depth)[0])
        return jnp.concatenate(results, axis=0)

    along_y = lax.map(plane_pass, potential)

    def column_block(block_index, carry):
        dual_part, density_part = carry
        start = (block_index * CY).astype(jnp.int32)
        logs = lax.dynamic_slice_in_dim(along_y, start, CY, axis=1)
        outer_field = lax.dynamic_slice_in_dim(external, start, CY, axis=1)
        new_dual, new_density = proximal(along_first(logs, depth), outer_field)
        return (lax.dynamic_update_slice_in_dim(dual_part, new_dual, start, axis=1),
                lax.dynamic_update_slice_in_dim(density_part, new_density, start, axis=1))

    zero_field = jnp.zeros((NZ, NY, NX), jnp.float32)
    dual_field, density_log = lax.fori_loop(0, NY // CY, column_block, (zero_field, zero_field))
    return dual_field, density_log
```

```python
import functools

import jax
import jax.numpy as jnp
import ml_dtypes
import numpy as np
from jax import lax
from jax.experimental import pallas as pl
from jax.experimental.pallas import tpu as pltpu
from jax.sharding import PartitionSpec as P

RADIUS = 128
BLOCK = 2 * RADIUS
LOWEST = -1e30

HIGHEST = lax.Precision.HIGHEST


def gauss(apart):
    apart = np.asarray(apart, np.float64)
    table = np.exp(-2.0 * apart * apart / float(RADIUS * RADIUS))
    return np.where(np.abs(apart) <= RADIUS, table, 0.0)


def two_terms(table):
    high = table.astype(ml_dtypes.bfloat16)
    low = (table - high.astype(np.float64)).astype(ml_dtypes.bfloat16)
    return high, low


def x_tables():
    table = gauss(np.arange(2 * BLOCK)[:, None] - RADIUS - np.arange(BLOCK)[None, :])
    return two_terms(table)


def y_table(rows):
    table = gauss(np.arange(rows + 2 * RADIUS)[None, :] - RADIUS - np.arange(rows)[:, None])
    return np.concatenate(two_terms(table), axis=0)


def split(weights):
    high = weights.astype(jnp.bfloat16)
    low = (weights - high.astype(jnp.float32)).astype(jnp.bfloat16)
    return high, low


def dot(a, b):
    return jnp.dot(a, b, preferred_element_type=jnp.float32)


def x_window(window, high_table, low_table):
    highest_value = jnp.max(window, axis=-1, keepdims=True)
    high, low = split(jnp.exp(window - highest_value))
    summed = dot(high, high_table) + (dot(low, high_table) + dot(high, low_table))
    return jnp.log(summed) + highest_value


def y_window(window, table):
    rows = table.shape[0] // 2
    highest_value = jnp.max(window, axis=0, keepdims=True)
    high, low = split(jnp.exp(window - highest_value))
    both = dot(table, high)
    summed = both[:rows] + (both[rows:] + dot(table[:rows], low))
    return jnp.log(summed) + highest_value


def proximal(logs, outer_field):
    shifted = logs - 0.5 * outer_field
    softer = jnp.maximum(shifted, 0.0) + jnp.log(1.0 + jnp.exp(-jnp.abs(shifted)))
    log_level = jnp.log(1.0 + softer)
    for newton_step in range(2):
        exp_level = jnp.exp(log_level)
        log_level = log_level - (log_level + exp_level - shifted) / (1.0 + exp_level)
    return log_level - logs, log_level


def slot_rows(place, slot, rows):
    return pl.ds(pl.multiple_of(lax.bitwise_xor(place, slot) * rows, rows), rows)


def params():
    return pltpu.CompilerParams(vmem_limit_bytes=48 * 1024 * 1024)


def cost(flops, count, transcendentals):
    return pl.CostEstimate(flops=int(flops), bytes_accessed=int(4 * count), transcendentals=int(transcendentals))


def x_kernel(first, last, slots, width, meta, *refs):
    refs = list(refs)
    main = refs.pop(0)
    left = None if first else refs.pop(0)
    right = None if last else refs.pop(0)
    high_ref, low_ref = refs.pop(0), refs.pop(0)
    outs = refs
    rows = main.shape[1]
    if slots:
        held = outs.pop()
    high_table, low_table = high_ref[...], low_ref[...]
    for j in range(width // BLOCK):
        begin, end = j * BLOCK - RADIUS, (j + 1) * BLOCK + RADIUS
        pieces = [main[0, :, max(begin, 0):min(end, width)]]
        table_from, table_to = 0, 2 * BLOCK
        if begin < 0:
            if first:
                table_from = RADIUS
            else:
                pieces.insert(0, left[0])
        if end > width:
            if last:
                table_to = 2 * BLOCK - RADIUS
            else:
                pieces.append(right[0])
        window = jnp.concatenate(pieces, axis=-1) if len(pieces) > 1 else pieces[0]
        result = x_window(window, high_table[table_from:table_to], low_table[table_from:table_to])
        columns = pl.ds(j * BLOCK, BLOCK)
        if slots:
            held[:, columns] = result
        else:
            outs[0][0, :, columns] = result
    if slots:
        for slot, out in enumerate(outs):
            out[0] = held[slot_rows(meta[0], slot, rows // slots), :]


def along_x(potential, meta, start, width, slots):
    depth, rows, length = potential.shape
    first, last = start == 0, start + width == length
    specs = [pl.BlockSpec((1, rows, width), lambda z, m: (z, 0, start // width))]
    if not first:
        specs.append(pl.BlockSpec((1, rows, RADIUS), lambda z, m: (z, 0, start // RADIUS - 1)))
    if not last:
        specs.append(pl.BlockSpec((1, rows, RADIUS), lambda z, m: (z, 0, (start + width) // RADIUS)))
    operands = [potential] * len(specs)
    for table in x_tables():
        specs.append(pl.BlockSpec(table.shape, lambda z, m: (0, 0)))
        operands.append(jnp.asarray(table))
    if slots:
        part = rows // slots
        outs = [jax.ShapeDtypeStruct((depth, part, width), jnp.float32)] * slots
        out_specs = [pl.BlockSpec((1, part, width), lambda z, m: (z, 0, 0))] * slots
        scratch = [pltpu.VMEM((rows, width), jnp.float32)]
    else:
        outs = jax.ShapeDtypeStruct((depth, rows, width), jnp.float32)
        out_specs = pl.BlockSpec((1, rows, width), lambda z, m: (z, 0, 0))
        scratch = []
    count = depth * rows * width
    return pl.pallas_call(
        functools.partial(x_kernel, first, last, slots, width),
        grid_spec=pltpu.PrefetchScalarGridSpec(
            num_scalar_prefetch=1, grid=(depth,), in_specs=specs, out_specs=out_specs, scratch_shapes=scratch
        ),
        out_shape=outs,
        compiler_params=params(),
        cost_estimate=cost(3 * 2 * 512 * count, 2 * count, 3 * count),
        name="along_x",
    )(meta, *operands)


def extended(meta, up, own, down):
    above = jnp.where(meta[1] == 1, -jnp.inf, up[0])
    below = jnp.where(meta[2] == 1, -jnp.inf, down[0])
    return jnp.concatenate([above, own[0], below], axis=0)


def y_slots_kernel(slots, meta, up, own, down, table, *refs):
    outs, held = refs[:slots], refs[slots]
    rows = own.shape[1]
    held[...] = y_window(extended(meta, up, own, down), table[...])
    for slot, out in enumerate(outs):
        out[0] = held[slot_rows(meta[0], slot, rows // slots), :]


def y_specs(rows, step):
    specs = [pl.BlockSpec((1, rows, step), lambda z, x, m: (z, 0, x))] * 3
    table = y_table(rows)
    specs.append(pl.BlockSpec(table.shape, lambda z, x, m: (0, 0)))
    return specs, jnp.asarray(table)


def along_y_slots(up, own, down, meta, slots):
    depth, rows, width = own.shape
    step = min(width, 512)
    specs, table = y_specs(rows, step)
    part = rows // slots
    count = own.size
    return pl.pallas_call(
        functools.partial(y_slots_kernel, slots),
        grid_spec=pltpu.PrefetchScalarGridSpec(
            num_scalar_prefetch=1,
            grid=(depth, width // step),
            in_specs=specs,
            out_specs=[pl.BlockSpec((1, part, step), lambda z, x, m: (z, 0, x))] * slots,
            scratch_shapes=[pltpu.VMEM((rows, step), jnp.float32)],
        ),
        out_shape=[jax.ShapeDtypeStruct((depth, part, width), jnp.float32)] * slots,
        compiler_params=params(),
        cost_estimate=cost(3 * 2 * 512 * count, 4 * count, 4 * count),
        name="along_y",
    )(meta, up, own, down, table)


def y_final_kernel(meta, up, own, down, table, outer, *refs):
    dual, density = refs[-2:]
    logs = y_window(extended(meta, up, own, down), table[...])
    dual[0], density[0] = proximal(logs, outer[0])


def along_y_final(up, own, down, external, meta, start, before):
    depth, rows, width = own.shape
    step = min(width, 512)
    specs, table = y_specs(rows, step)
    place = pl.BlockSpec((1, rows, step), lambda z, x, m: (z, 0, x + start // step))
    specs.append(place)
    count = own.size
    shape = jax.ShapeDtypeStruct(external.shape, jnp.float32)
    specs += [pl.BlockSpec(memory_space=pl.ANY)] * len(before)
    return pl.pallas_call(
        y_final_kernel,
        grid_spec=pltpu.PrefetchScalarGridSpec(
            num_scalar_prefetch=1, grid=(depth, width // step), in_specs=specs, out_specs=[place, place]
        ),
        out_shape=[shape, shape],
        input_output_aliases={6 + i: i for i in range(len(before))},
        compiler_params=params(),
        cost_estimate=cost(3 * 2 * 512 * count, 6 * count, 12 * count),
        name="along_y_proximal",
    )(meta, up, own, down, table, external, *before)


def z_kernel(slots, depth, table, *refs):
    ins, outs = refs[:slots], refs[slots:]
    rows, width = ins[0].shape[1:]
    total = slots * depth

    def step(i, carry):
        columns = pl.ds(pl.multiple_of(i * 128, 128), 128)
        values = [ins[k // depth][k % depth, :, columns] for k in range(total)]
        highest_value = jnp.maximum(functools.reduce(jnp.maximum, values), LOWEST)
        weights = [jnp.exp(value - highest_value) for value in values]
        for o in range(total):
            summed = weights[0] * table[o, 0]
            for k in range(1, total):
                summed = summed + weights[k] * table[o, k]
            outs[o // depth][o % depth, :, columns] = jnp.log(summed) + highest_value
        return carry

    lax.fori_loop(0, width // 128, step, 0)


def z_table(place, slots, depth):
    cell = jnp.arange(slots * depth)
    cell = lax.bitwise_xor(cell // depth, place) * depth + cell % depth
    apart = cell[:, None] - cell[None, :]
    distance = apart.astype(jnp.float32)
    values = jnp.exp(-2.0 * distance * distance / float(RADIUS * RADIUS))
    return jnp.where(jnp.abs(apart) <= RADIUS, values, 0.0)


def along_z(parts, table):
    slots = len(parts)
    depth, rows, width = parts[0].shape
    count = slots * parts[0].size
    step = min(width, 512)
    spec = pl.BlockSpec((depth, rows, step), lambda x: (0, 0, x))
    return pl.pallas_call(
        functools.partial(z_kernel, slots, depth),
        grid=(width // step,),
        in_specs=[pl.BlockSpec(memory_space=pltpu.SMEM)] + [spec] * slots,
        out_specs=[spec] * slots,
        out_shape=[jax.ShapeDtypeStruct(parts[0].shape, jnp.float32)] * slots,
        compiler_params=params(),
        cost_estimate=cost(50 * count, 2 * count, 2 * count),
        name="along_z",
    )(table, *parts)


def join_kernel(slots, meta, *refs):
    ins, out = refs[:slots], refs[slots]
    rows = ins[0].shape[1]
    for slot, part in enumerate(ins):
        out[0, slot_rows(meta[0], slot, rows), :] = part[0]


def join(parts, meta):
    slots = len(parts)
    depth, part, width = parts[0].shape
    spec = pl.BlockSpec((1, part, width), lambda z, m: (z, 0, 0))
    shape = (depth, slots * part, width)
    return pl.pallas_call(
        functools.partial(join_kernel, slots),
        grid_spec=pltpu.PrefetchScalarGridSpec(
            num_scalar_prefetch=1,
            grid=(depth,),
            in_specs=[spec] * slots,
            out_specs=pl.BlockSpec((1,) + shape[1:], lambda z, m: (z, 0, 0)),
        ),
        out_shape=jax.ShapeDtypeStruct(shape, jnp.float32),
        compiler_params=params(),
        cost_estimate=cost(0, 2 * depth * slots * part * width, 0),
        name="join",
    )(meta, *parts)


def final_kernel(slots, meta, *refs):
    ins, outer = refs[:slots], refs[slots]
    dual, density = refs[-2:]
    rows = ins[0].shape[1]
    for slot, part in enumerate(ins):
        here = slot_rows(meta[0], slot, rows)
        dual[0, here, :], density[0, here, :] = proximal(part[0], outer[0, here, :])


def final(parts, external, meta, start, before):
    slots = len(parts)
    depth, part, width = parts[0].shape
    step = min(width, 512)
    place = pl.BlockSpec((1, slots * part, step), lambda z, x, m: (z, 0, x + start // step))
    specs = [pl.BlockSpec((1, part, step), lambda z, x, m: (z, 0, x))] * slots + [place]
    specs += [pl.BlockSpec(memory_space=pl.ANY)] * len(before)
    shape = jax.ShapeDtypeStruct(external.shape, jnp.float32)
    count = slots * parts[0].size
    return pl.pallas_call(
        functools.partial(final_kernel, slots),
        grid_spec=pltpu.PrefetchScalarGridSpec(
            num_scalar_prefetch=1, grid=(depth, width // step), in_specs=specs, out_specs=[place, place]
        ),
        out_shape=[shape, shape],
        input_output_aliases={2 + slots + i: i for i in range(len(before))},
        compiler_params=params(),
        cost_estimate=cost(40 * count, 4 * count, 8 * count),
        name="proximal",
    )(meta, *parts, external, *before)


def neighbours(cells):
    ends = lax.axis_size("gy") - 1
    up = lax.ppermute(cells, "gy", [(i, i + 1) for i in range(ends)])
    down = lax.ppermute(cells, "gy", [(i + 1, i) for i in range(ends)])
    return up, down


def exchange(parts):
    count = len(parts)
    order = sorted(range(1, count), key=lambda s: -bin(s).count("1"))
    moved = dict((s, lax.ppermute(parts[s], "gz", [(i, i ^ s) for i in range(count)])) for s in order)
    return [parts[0]] + [moved[s] for s in range(1, count)]


def in_parts(potential, external):
    slots = lax.axis_size("gz")
    depth, rows, length = potential.shape
    half = length // 2
    place, row_place = lax.axis_index("gz"), lax.axis_index("gy")
    meta = jnp.stack(
        [place, (row_place == 0).astype(jnp.int32), (row_place == lax.axis_size("gy") - 1).astype(jnp.int32)]
    ).astype(jnp.int32)
    table = z_table(place, slots, depth)

    parts = along_x(potential, meta, half, half, slots)
    own = along_x(potential, meta, 0, half, 0)
    up, down = neighbours(own)
    parts = exchange(parts)
    parts = along_z(parts, table)
    parts = exchange(parts)
    later = join(parts, meta)
    later_up, later_down = neighbours(later)
    parts = along_y_slots(up, own, down, meta, slots)
    parts = exchange(parts)
    parts = along_z(parts, table)
    parts = exchange(parts)
    outs = along_y_final(later_up, later, later_down, external, meta, half, [])
    return tuple(final(parts, external, meta, 0, outs))


def whole(potential, external):
    depth = RADIUS
    slots = lax.axis_size("gz")
    position, devices = lax.axis_index("gy"), lax.axis_size("gy")
    planes, rows, length = potential.shape

    def table(in_index, out_index):
        apart = in_index[:, None] - out_index[None, :]
        distance = apart.astype(jnp.float32)
        values = jnp.exp(-2.0 * distance * distance / float(RADIUS * RADIUS))
        return jnp.where(jnp.abs(apart) <= RADIUS, values, 0.0)

    def summed(equation, window, axis, kernel):
        highest_value = jnp.max(window, axis=axis, keepdims=True)
        weights = jnp.exp(window - highest_value)
        return jnp.log(jnp.einsum(equation, weights, kernel, precision=HIGHEST)) + highest_value

    border = jnp.full((planes, rows, depth), -jnp.inf, jnp.float32)
    padded = jnp.concatenate([border, potential, border], axis=-1)
    pieces = padded.reshape(planes, rows, length // BLOCK + 1, BLOCK)
    window = jnp.concatenate([pieces[..., :-1, :], pieces[..., 1:, :]], axis=-1)
    kernel = table(jnp.arange(2 * BLOCK) - depth, jnp.arange(BLOCK))
    logs = summed("...w,wo->...o", window, -1, kernel).reshape(potential.shape)

    up, down = neighbours(logs)
    up = jnp.where(position == 0, -jnp.inf, up[:, rows - depth:])
    down = jnp.where(position == devices - 1, -jnp.inf, down[:, :depth])
    window = jnp.concatenate([up, logs, down], axis=1)
    kernel = table(jnp.arange(rows + 2 * depth) - depth, jnp.arange(rows))
    logs = summed("zwx,wo->zox", window, 1, kernel)

    logs = lax.all_to_all(logs, "gz", split_axis=1, concat_axis=0, tiled=True)
    cells = jnp.arange(slots * planes)
    logs = summed("wyx,wo->oyx", logs, 0, table(cells, cells))
    logs = lax.all_to_all(logs, "gz", split_axis=0, concat_axis=1, tiled=True)
    return proximal(logs, external)


def local(potential, external):
    slots = lax.axis_size("gz")
    depth, rows, length = potential.shape
    if slots & (slots - 1) == 0 and rows % (8 * slots) == 0 and slots * depth <= 32 and length % (4 * BLOCK) == 0 and rows == RADIUS:
        return in_parts(potential, external)
    return whole(potential, external)


def solution(mesh):
    return jax.shard_map(
        local,
        mesh=mesh,
        in_specs=(P("gz", "gy", None), P("gz", "gy", None)),
        out_specs=(P("gz", "gy", None), P("gz", "gy", None)),
        check_vma=False,
    )
```

```python
import functools

import jax
import jax.numpy as jnp
import ml_dtypes
import numpy as np
from jax import lax
from jax.experimental import pallas as pl
from jax.experimental.pallas import tpu as pltpu
from jax.sharding import PartitionSpec as P

RADIUS = 128
BLOCK = 2 * RADIUS
VMEM_BYTES = 24 * 1024 * 1024
LOWEST = -1e30

HIGHEST = lax.Precision.HIGHEST


def gauss(apart):
    apart = np.asarray(apart, np.float64)
    table = np.exp(-2.0 * apart * apart / float(RADIUS * RADIUS))
    return np.where(np.abs(apart) <= RADIUS, table, 0.0)


def two_terms(table):
    high = table.astype(ml_dtypes.bfloat16)
    low = (table - high.astype(np.float64)).astype(ml_dtypes.bfloat16)
    return high, low


def x_tables():
    table = gauss(np.arange(2 * BLOCK)[:, None] - RADIUS - np.arange(BLOCK)[None, :])
    return two_terms(table)


def y_table(rows):
    table = gauss(np.arange(rows + 2 * RADIUS)[None, :] - RADIUS - np.arange(rows)[:, None])
    before, own, behind = np.split(table, [RADIUS, RADIUS + rows], axis=1)
    tables = [[behind, own, before], [before, own, behind]]
    return np.concatenate([term for blocks in tables for term in two_terms(np.concatenate(blocks, axis=1))], axis=0)


def split(weights):
    high = weights.astype(jnp.bfloat16)
    low = (weights - high.astype(jnp.float32)).astype(jnp.bfloat16)
    return high, low


def dot(a, b):
    return jnp.dot(a, b, preferred_element_type=jnp.float32)


def x_window(window, high_table, low_table):
    highest_value = jnp.max(window, axis=-1, keepdims=True)
    high, low = split(jnp.exp(window - highest_value))
    summed = dot(high, high_table) + (dot(low, high_table) + dot(high, low_table))
    return jnp.log(summed) + highest_value


def two_term_sum(table, weights):
    rows = table.shape[0] // 2
    high, low = split(weights)
    both = dot(table, high)
    return both[:rows] + (both[rows:] + dot(table[:rows], low))


def y_window(window, table):
    highest_value = jnp.max(window, axis=0, keepdims=True)
    return jnp.log(two_term_sum(table, jnp.exp(window - highest_value))) + highest_value


def proximal(logs, outer_field):
    shifted = logs - 0.5 * outer_field
    level = 1.0 + (jnp.maximum(shifted, 0.0) + jnp.log(1.0 + jnp.exp(-jnp.abs(shifted))))
    log_level = jnp.log(level)
    for newton_step in range(2):
        if newton_step:
            level = jnp.exp(log_level)
        log_level = (level * (log_level - 1.0) + shifted) / (1.0 + level)
    return log_level - logs, log_level


def slot_rows(place, slot, rows):
    return pl.ds(pl.multiple_of(lax.bitwise_xor(place, slot) * rows, rows), rows)


def all_of(array):
    return pl.BlockSpec(array.shape, lambda i, m: (0,) * array.ndim)


def call(kernel, name, meta, operands, outs, work, aliases={}, scratch=(), after=(), after_far=False, in_place=False):
    used = 1 + len(operands)
    if after_far:
        after = [pltpu.with_memory_space_constraint(array, pltpu.HBM) for array in after]
    operands = operands + [(array, pl.BlockSpec(memory_space=pl.ANY)) for array in after]

    def body(*refs):
        kernel(*refs[:used], *refs[used + len(after) :])

    shapes = [jax.ShapeDtypeStruct(shape, jnp.float32) for shape in outs]
    return pl.pallas_call(
        body,
        grid_spec=pltpu.PrefetchScalarGridSpec(
            num_scalar_prefetch=1,
            grid=(1,),
            in_specs=[spec for _, spec in operands],
            out_specs=[pl.BlockSpec(memory_space=pltpu.HBM) if in_place else all_of(shape) for shape in shapes],
            scratch_shapes=list(scratch),
        ),
        out_shape=shapes,
        input_output_aliases=aliases,
        compiler_params=pltpu.CompilerParams(vmem_limit_bytes=VMEM_BYTES),
        cost_estimate=pl.CostEstimate(
            flops=2 * work[0], bytes_accessed=8 * sum(int(np.prod(shape)) for shape in outs), transcendentals=work[1]
        ),
        name=name,
    )(meta, *[array for array, _ in operands])


def x_kernel(edges, received, parts, meta, main, left, right, high_ref, low_ref, *refs):
    refs = list(refs)
    other = refs.pop(0) if received else None
    held = refs.pop() if parts else None
    depth, rows, width = main.shape
    own = slice(0, depth)

    def ended(edge, which):
        return jnp.where(meta[3] == which - 1, -jnp.inf, edge) if which else edge

    cells = [ended(left[...], edges[0]), main[...], ended(right[...], edges[1])]
    cells = jnp.concatenate([piece.reshape(depth * rows, piece.shape[-1]) for piece in cells], axis=-1)
    for j in range(width // BLOCK):
        window = cells[:, j * BLOCK : (j + 2) * BLOCK]
        result = x_window(window, high_ref[...], low_ref[...]).reshape(depth, rows, BLOCK)
        columns = pl.ds(j * BLOCK, BLOCK)
        if parts:
            held[:, :, columns] = result
        else:
            refs[0][own, :, columns] = result
    if parts:
        for slot, out in enumerate(refs):
            here = slot_rows(meta[0], slot, rows // parts)
            out[own] = held[:, here, :]
            out[depth:] = other[:, here, :]
    elif received:
        refs[0][depth:] = other[...]


def along_x(potential, meta, mine, start, width, parts, received=None, after=(), far=False):
    depth, rows, length = potential.shape
    half = length // 2

    def begin(m, unit):
        return (m[3] if mine else 1 - m[3]) * (half // unit) + start // unit

    edges = (0 if start else (1 if mine else 2)), (0 if start + width < half else (2 if mine else 1))
    before = lambda i, m: (0, 0, jnp.maximum(begin(m, RADIUS) - 1, 0))
    behind = lambda i, m: (0, 0, jnp.minimum(begin(m, RADIUS) + width // RADIUS, length // RADIUS - 1))
    operands = [
        (potential, pl.BlockSpec((depth, rows, width), lambda i, m: (0, 0, begin(m, width)))),
        (potential, pl.BlockSpec((depth, rows, RADIUS), before)),
        (potential, pl.BlockSpec((depth, rows, RADIUS), behind)),
    ]
    operands += [(jnp.asarray(table), all_of(table)) for table in x_tables()]
    if far:
        operands = [(pltpu.with_memory_space_constraint(array, pltpu.HBM), spec) for array, spec in operands]
    planes = depth
    if received is not None:
        planes = 2 * depth
        operands.append((received, all_of(received)))
    outs = [(planes, rows // parts, width)] * parts if parts else [(planes, rows, width)]
    count = depth * rows * width
    return call(
        functools.partial(x_kernel, edges, received is not None, parts),
        "along_x", meta, operands, outs, (6 * BLOCK * count, 3 * count),
        scratch=[pltpu.VMEM((depth, rows, width), jnp.float32)] if parts else [], after=after,
    )


def along_y(meta, cells, plane, table):
    paired, own, other = cells
    cells = [
        jnp.where(meta[1] == 1, -jnp.inf, paired[plane]),
        own[plane],
        jnp.where(meta[2] == 1, -jnp.inf, other[plane]),
    ]
    return y_window(jnp.concatenate(cells, axis=0), table[...])


def y_operands(cells, planes, first=0):
    rows, width = cells[1].shape[1:]
    operands = [(array, pl.BlockSpec((planes, rows, width), lambda i, m: (first // planes, 0, 0))) for array in cells]
    table = y_table(rows)
    return operands + [(jnp.asarray(table), pl.BlockSpec((2 * rows, table.shape[1]), lambda i, m: (m[4], 0)))]


def y_work(count):
    return 12 * RADIUS * count, 4 * count


def y_parts_kernel(meta, paired, own, other, table, *refs):
    outs, held = refs[:-1], refs[-1]
    planes, rows, width = own.shape
    for plane in range(planes):
        held[plane] = along_y(meta, (paired, own, other), plane, table)
    for slot, out in enumerate(outs):
        out[...] = held[:, slot_rows(meta[0], slot, rows // len(outs)), :]


def along_y_parts(cells, meta, parts, after=()):
    planes, rows, width = cells[1].shape
    return call(
        y_parts_kernel, "along_y", meta, y_operands(cells, planes), [(planes, rows // parts, width)] * parts,
        y_work(cells[1].size), scratch=[pltpu.VMEM((planes, rows, width), jnp.float32)], after=after,
    )


def y_send_kernel(meta, paired, own, other, table, out):
    for plane in range(out.shape[0]):
        out[plane] = along_y(meta, (paired, own, other), plane, table)


def along_y_send(cells, meta, first, after=()):
    planes, rows, width = cells[1].shape
    planes -= first
    return call(
        y_send_kernel, "along_y", meta, y_operands(cells, planes, first), [(planes, rows, width)], y_work(cells[1].size // 2),
        after=after,
    )[0]


def z_kernel(meta, table, *refs):
    count = len(refs) // 2
    ins, outs = refs[:count], refs[count:]
    planes, rows, width = ins[0].shape
    kernel = table[...]
    for tile in range(rows // 8):
        here = pl.ds(8 * tile, 8)
        for begin in range(0, width, BLOCK):
            columns = pl.ds(begin, min(BLOCK, width - begin))
            values = [part[k, here, columns] for part in ins for k in range(planes)]
            highest_value = jnp.maximum(functools.reduce(jnp.maximum, values), LOWEST)
            weights = jnp.concatenate([jnp.exp(value - highest_value) for value in values], axis=0)
            logs = jnp.log(two_term_sum(kernel, weights))
            for o in range(count * planes):
                outs[o // planes][o % planes, here, columns] = logs[8 * o : 8 * o + 8] + highest_value


def z_table(place, slots, depth):
    cell = jnp.arange(slots * depth * 8) // 8
    row = jnp.arange(slots * depth * 8) % 8
    cell = lax.bitwise_xor(cell // depth, place) * depth + cell % depth
    apart = cell[:, None] - cell[None, :]
    distance = apart.astype(jnp.float32)
    values = jnp.exp(-2.0 * distance * distance / float(RADIUS * RADIUS))
    values = jnp.where((jnp.abs(apart) <= RADIUS) & (row[:, None] == row[None, :]), values, 0.0)
    high = lax.reduce_precision(values, 8, 7)
    return jnp.concatenate([high, values - high], axis=0).astype(jnp.bfloat16)


def along_z(parts, table, meta):
    count = len(parts) * parts[0].size
    return call(
        z_kernel, "along_z", meta, [(array, all_of(array)) for array in [table] + parts], [part.shape for part in parts],
        (768 * count, 2 * count),
    )


def join_kernel(meta, *refs):
    ins, out = refs[:-1], refs[-1]
    for slot, part in enumerate(ins):
        out[:, slot_rows(meta[0], slot, part.shape[1]), :] = part[...]


def join(parts, meta, first=0, after=(), after_far=False):
    planes, part, width = parts[0].shape
    block = planes - first
    spec = pl.BlockSpec((block, part, width), lambda i, m: (first // block, 0, 0))
    return call(
        join_kernel, "join", meta, [(array, spec) for array in parts], [(block, part * len(parts), width)], (0, 0), after=after,
        after_far=after_far,
    )[0]


def final_kernel(pieces, meta, *refs):
    refs = list(refs)
    ins = [[refs.pop(0) for _ in range(count + 1)] for count, _, _ in pieces]
    results, sems = refs[-1 - len(pieces) : -1], refs[-1]
    outs = refs[-3 - len(pieces) : -1 - len(pieces)]
    depth = ins[0][-1].shape[0]
    half = outs[0].shape[2] // 2
    copies = []
    for at, (count, mine, start) in enumerate(pieces):
        cells, outer, held = ins[at][:-1], ins[at][-1], results[at]
        width = outer.shape[2]
        column = pl.multiple_of((meta[3] if mine else 1 - meta[3]) * half + start, width)
        for plane in range(depth):
            if count == 4 and cells[0].shape == outer.shape:
                logs = along_y(meta, cells[:3], plane, cells[3])
                held[0, plane], held[1, plane] = proximal(logs, outer[plane])
            elif count == 1:
                held[0, plane], held[1, plane] = proximal(cells[0][plane], outer[plane])
            else:
                for slot, part in enumerate(cells):
                    here = slot_rows(meta[0], slot, part.shape[1])
                    held[0, plane, here, :], held[1, plane, here, :] = proximal(part[plane], outer[plane, here, :])
            for k, out in enumerate(outs):
                copies.append(
                    pltpu.make_async_copy(
                        held.at[k, plane], out.at[plane, :, pl.ds(column, width)], sems.at[2 * (at * depth + plane) + k]
                    )
                )
                copies[-1].start()
    for copy in copies:
        copy.wait()


def final(pieces, external, meta, before):
    depth, rows, length = external.shape
    operands, kinds, scratch, size = [], [], [], 0
    for given, mine, start in pieces:
        width = given[0][0].shape[2]
        place = lambda i, m, mine=mine, start=start, width=width: (0, 0, ((m[3] if mine else 1 - m[3]) * (length // 2) + start) // width)
        operands += given + [(external, pl.BlockSpec((depth, rows, width), place))]
        kinds.append((len(given), mine, start))
        scratch.append(pltpu.VMEM((2, depth, rows, width), jnp.float32))
        size += depth * rows * width
    aliases = {1 + len(operands) + i: i for i in range(len(before))}
    operands += [(array, pl.BlockSpec(memory_space=pltpu.HBM)) for array in before]
    return call(
        functools.partial(final_kernel, kinds), "proximal", meta, operands, [external.shape] * 2, (20 * size, 6 * size),
        aliases, scratch + [pltpu.SemaphoreType.DMA((2 * depth * len(pieces),))], in_place=True,
    )


def own_planes(arrays, depth):
    return [(array, pl.BlockSpec((depth,) + array.shape[1:], lambda i, m: (0, 0, 0))) for array in arrays]


def pairs(count, first):
    ends = [(i, i + 1) for i in range(first, count - 1, 2)]
    return ends + [(j, i) for i, j in ends]


def neighbours(cells):
    count = lax.axis_size("gy")
    return lax.ppermute(cells, "gy", pairs(count, 0)), cells, lax.ppermute(cells, "gy", pairs(count, 1))


def row_meta():
    place, count = lax.axis_index("gy"), lax.axis_size("gy")
    odd = place % 2
    return [place + 1 - odd >= count, (place == 0) | (place + odd >= count), odd]


def swap(cells, bits):
    return lax.ppermute(cells, "gz", [(i, i ^ bits) for i in range(lax.axis_size("gz"))])


def exchange(parts):
    order = sorted(range(1, len(parts)), key=lambda r: -bin(r).count("1"))
    moved = dict((r, swap(parts[r], 2 * r)) for r in order)
    return [parts[0]] + [moved[r] for r in range(1, len(parts))]


def in_parts(potential, external):
    slots = lax.axis_size("gz")
    depth, rows, length = potential.shape
    parts = slots // 2
    place = lax.axis_index("gz")
    first_missing, second_missing, odd = row_meta()
    meta = jnp.stack([place // 2, first_missing, second_missing, place % 2, odd]).astype(jnp.int32)
    table = z_table(place, slots, depth)

    width = length // 4
    first = along_x(potential, meta, False, 0, width, 0, far=True)[0]
    later = along_x(potential, meta, False, width, width, 0, after=[first])[0]
    first = along_x(potential, meta, True, 0, width, 0, swap(first, 1))[0]
    later = along_x(potential, meta, True, width, width, parts, swap(later, 1), after=[first])

    first = neighbours(first)
    later = exchange(later)
    later = along_z(later, table, meta)
    first = along_y_parts(first, meta, parts)
    later = join(exchange(later), meta, after=first)
    later = neighbours(later)
    first = exchange(first)
    first = along_z(first, table, meta)
    later_other = swap(along_y_send(later, meta, depth, after=first), 1)
    first = exchange(first)

    outs = final([(y_operands(later, depth), True, width)], external, meta, [])
    first_other = swap(join(first, meta, depth, after=outs, after_far=True), 1)
    other = (own_planes([later_other], depth), False, width)
    own = (own_planes(first, depth), True, 0)
    outs = final([other, own], external, meta, outs)
    return tuple(final([(own_planes([first_other], depth), False, 0)], external, meta, outs))


def whole(potential, external):
    depth = RADIUS
    slots = lax.axis_size("gz")
    position, devices = lax.axis_index("gy"), lax.axis_size("gy")
    planes, rows, length = potential.shape

    def table(in_index, out_index):
        apart = in_index[:, None] - out_index[None, :]
        distance = apart.astype(jnp.float32)
        values = jnp.exp(-2.0 * distance * distance / float(RADIUS * RADIUS))
        return jnp.where(jnp.abs(apart) <= RADIUS, values, 0.0)

    def summed(equation, window, axis, kernel):
        highest_value = jnp.max(window, axis=axis, keepdims=True)
        weights = jnp.exp(window - highest_value)
        return jnp.log(jnp.einsum(equation, weights, kernel, precision=HIGHEST)) + highest_value

    border = jnp.full((planes, rows, depth), -jnp.inf, jnp.float32)
    padded = jnp.concatenate([border, potential, border], axis=-1)
    pieces = padded.reshape(planes, rows, length // BLOCK + 1, BLOCK)
    window = jnp.concatenate([pieces[..., :-1, :], pieces[..., 1:, :]], axis=-1)
    kernel = table(jnp.arange(2 * BLOCK) - depth, jnp.arange(BLOCK))
    logs = summed("...w,wo->...o", window, -1, kernel).reshape(potential.shape)

    paired, _, other = neighbours(logs)
    up, down = jnp.where(position % 2 == 0, other, paired), jnp.where(position % 2 == 0, paired, other)
    up = jnp.where(position == 0, -jnp.inf, up[:, rows - depth :])
    down = jnp.where(position == devices - 1, -jnp.inf, down[:, :depth])
    window = jnp.concatenate([up, logs, down], axis=1)
    kernel = table(jnp.arange(rows + 2 * depth) - depth, jnp.arange(rows))
    logs = summed("zwx,wo->zox", window, 1, kernel)

    logs = lax.all_to_all(logs, "gz", split_axis=1, concat_axis=0, tiled=True)
    cells = jnp.arange(slots * planes)
    logs = summed("wyx,wo->oyx", logs, 0, table(cells, cells))
    logs = lax.all_to_all(logs, "gz", split_axis=0, concat_axis=1, tiled=True)
    return proximal(logs, external)


def local(potential, external):
    slots = lax.axis_size("gz")
    depth, rows, length = potential.shape
    tiles = slots > 2 and slots & (slots - 1) == 0 and rows % (4 * slots) == 0 and slots * depth <= 32
    if tiles and rows == RADIUS and length % (4 * BLOCK) == 0:
        return in_parts(potential, external)
    return whole(potential, external)


def solution(mesh):
    return jax.shard_map(
        local,
        mesh=mesh,
        in_specs=(P("gz", "gy", None), P("gz", "gy", None)),
        out_specs=(P("gz", "gy", None), P("gz", "gy", None)),
        check_vma=False,
    )
```

```python
import functools

import jax
import jax.numpy as jnp
import ml_dtypes
import numpy as np
from jax import lax
from jax.experimental import pallas as pl
from jax.experimental.pallas import tpu as pltpu
from jax.sharding import PartitionSpec as P

RADIUS = 128
BLOCK = 2 * RADIUS
VMEM_BYTES = 24 * 1024 * 1024
FIRST_CUTS, LATER_CUTS = 1, 1
LOWEST = -1e30

HIGHEST = lax.Precision.HIGHEST


def gauss(apart):
    apart = np.asarray(apart, np.float64)
    table = np.exp(-2.0 * apart * apart / float(RADIUS * RADIUS))
    return np.where(np.abs(apart) <= RADIUS, table, 0.0)


def two_terms(table):
    high = table.astype(ml_dtypes.bfloat16)
    low = (table - high.astype(np.float64)).astype(ml_dtypes.bfloat16)
    return high, low


def x_tables():
    table = gauss(np.arange(2 * BLOCK)[:, None] - RADIUS - np.arange(BLOCK)[None, :])
    return two_terms(table)


def y_table(rows):
    table = gauss(np.arange(rows + 2 * RADIUS)[None, :] - RADIUS - np.arange(rows)[:, None])
    before, own, behind = np.split(table, [RADIUS, RADIUS + rows], axis=1)
    tables = [[behind, own, before], [before, own, behind]]
    return np.concatenate([term for blocks in tables for term in two_terms(np.concatenate(blocks, axis=1))], axis=0)


def split(weights):
    high = weights.astype(jnp.bfloat16)
    low = (weights - high.astype(jnp.float32)).astype(jnp.bfloat16)
    return high, low


def dot(a, b):
    return jnp.dot(a, b, preferred_element_type=jnp.float32)


def x_window(window, high_table, low_table):
    highest_value = jnp.max(window, axis=-1, keepdims=True)
    high, low = split(jnp.exp(window - highest_value))
    summed = dot(high, high_table) + (dot(low, high_table) + dot(high, low_table))
    return jnp.log(summed) + highest_value


def two_term_sum(table, weights):
    rows = table.shape[0] // 2
    high, low = split(weights)
    both = dot(table, high)
    return both[:rows] + (both[rows:] + dot(table[:rows], low))


def y_window(window, table):
    highest_value = jnp.max(window, axis=0, keepdims=True)
    return jnp.log(two_term_sum(table, jnp.exp(window - highest_value))) + highest_value


def proximal(logs, outer_field):
    shifted = logs - 0.5 * outer_field
    level = 1.0 + (jnp.maximum(shifted, 0.0) + jnp.log(1.0 + jnp.exp(-jnp.abs(shifted))))
    log_level = jnp.log(level)
    for newton_step in range(2):
        if newton_step:
            level = jnp.exp(log_level)
        log_level = (level * (log_level - 1.0) + shifted) / (1.0 + level)
    return log_level - logs, log_level


def slot_rows(place, slot, rows):
    return pl.ds(pl.multiple_of(lax.bitwise_xor(place, slot) * rows, rows), rows)


def tiles(place, parts, rows):
    part, width = parts[0].shape[1:]
    count = rows // part
    return [(slot_rows(place, at % count, part), pl.ds(at // count * width, width)) for at in range(len(parts))]


def all_of(array):
    return pl.BlockSpec(array.shape, lambda i, m: (0,) * array.ndim)


def call(kernel, name, meta, operands, outs, work, aliases={}, scratch=(), after=(), after_far=False, in_place=False):
    used = 1 + len(operands)
    if after_far:
        after = [pltpu.with_memory_space_constraint(array, pltpu.HBM) for array in after]
    operands = operands + [(array, pl.BlockSpec(memory_space=pl.ANY)) for array in after]

    def body(*refs):
        kernel(*refs[:used], *refs[used + len(after) :])

    shapes = [jax.ShapeDtypeStruct(shape, jnp.float32) for shape in outs]
    return pl.pallas_call(
        body,
        grid_spec=pltpu.PrefetchScalarGridSpec(
            num_scalar_prefetch=1,
            grid=(1,),
            in_specs=[spec for _, spec in operands],
            out_specs=[pl.BlockSpec(memory_space=pltpu.HBM) if in_place else all_of(shape) for shape in shapes],
            scratch_shapes=list(scratch),
        ),
        out_shape=shapes,
        input_output_aliases=aliases,
        compiler_params=pltpu.CompilerParams(vmem_limit_bytes=VMEM_BYTES),
        cost_estimate=pl.CostEstimate(
            flops=2 * work[0], bytes_accessed=8 * sum(int(np.prod(shape)) for shape in outs), transcendentals=work[1]
        ),
        name=name,
    )(meta, *[array for array, _ in operands])


def x_kernel(edges, received, parts, meta, main, left, right, high_ref, low_ref, *refs):
    refs = list(refs)
    other = refs.pop(0) if received else None
    held = refs.pop() if parts else None
    depth, rows, width = main.shape
    own = slice(0, depth)

    def ended(edge, which):
        return jnp.where(meta[3] == which - 1, -jnp.inf, edge) if which else edge

    cells = [ended(left[...], edges[0]), main[...], ended(right[...], edges[1])]
    cells = jnp.concatenate([piece.reshape(depth * rows, piece.shape[-1]) for piece in cells], axis=-1)
    for j in range(width // BLOCK):
        window = cells[:, j * BLOCK : (j + 2) * BLOCK]
        result = x_window(window, high_ref[...], low_ref[...]).reshape(depth, rows, BLOCK)
        columns = pl.ds(j * BLOCK, BLOCK)
        if parts:
            held[:, :, columns] = result
        else:
            refs[0][own, :, columns] = result
    if parts:
        for out, (here, columns) in zip(refs, tiles(meta[0], refs, rows)):
            out[own] = held[:, here, columns]
            out[depth:] = other[:, here, columns]
    elif received:
        refs[0][depth:] = other[...]


def along_x(potential, meta, mine, start, width, parts, received=None, cuts=1, after=(), far=False):
    depth, rows, length = potential.shape
    half = length // 2

    def begin(m, unit):
        return (m[3] if mine else 1 - m[3]) * (half // unit) + start // unit

    edges = (0 if start else (1 if mine else 2)), (0 if start + width < half else (2 if mine else 1))
    before = lambda i, m: (0, 0, jnp.maximum(begin(m, RADIUS) - 1, 0))
    behind = lambda i, m: (0, 0, jnp.minimum(begin(m, RADIUS) + width // RADIUS, length // RADIUS - 1))
    operands = [
        (potential, pl.BlockSpec((depth, rows, width), lambda i, m: (0, 0, begin(m, width)))),
        (potential, pl.BlockSpec((depth, rows, RADIUS), before)),
        (potential, pl.BlockSpec((depth, rows, RADIUS), behind)),
    ]
    operands += [(jnp.asarray(table), all_of(table)) for table in x_tables()]
    if far:
        operands = [(pltpu.with_memory_space_constraint(array, pltpu.HBM), spec) for array, spec in operands]
    planes = depth
    if received is not None:
        planes = 2 * depth
        operands.append((received, all_of(received)))
    outs = [(planes, rows // parts, width // cuts)] * (parts * cuts) if parts else [(planes, rows, width)]
    count = depth * rows * width
    return call(
        functools.partial(x_kernel, edges, received is not None, parts),
        "along_x", meta, operands, outs, (6 * BLOCK * count, 3 * count),
        scratch=[pltpu.VMEM((depth, rows, width), jnp.float32)] if parts else [], after=after,
    )


def along_y(meta, cells, plane, table):
    paired, own, other = cells
    cells = [
        jnp.where(meta[1] == 1, -jnp.inf, paired[plane]),
        own[plane],
        jnp.where(meta[2] == 1, -jnp.inf, other[plane]),
    ]
    return y_window(jnp.concatenate(cells, axis=0), table[...])


def y_operands(cells, planes, first=0):
    rows, width = cells[1].shape[1:]
    operands = [(array, pl.BlockSpec((planes, rows, width), lambda i, m: (first // planes, 0, 0))) for array in cells]
    table = y_table(rows)
    return operands + [(jnp.asarray(table), pl.BlockSpec((2 * rows, table.shape[1]), lambda i, m: (m[4], 0)))]


def y_work(count):
    return 12 * RADIUS * count, 4 * count


def y_parts_kernel(meta, paired, own, other, table, *refs):
    outs, held = refs[:-1], refs[-1]
    planes, rows, width = own.shape
    for plane in range(planes):
        held[plane] = along_y(meta, (paired, own, other), plane, table)
    for out, (here, columns) in zip(outs, tiles(meta[0], outs, rows)):
        out[...] = held[:, here, columns]


def along_y_parts(cells, meta, parts, cuts=1, after=()):
    planes, rows, width = cells[1].shape
    return call(
        y_parts_kernel, "along_y", meta, y_operands(cells, planes), [(planes, rows // parts, width // cuts)] * (parts * cuts),
        y_work(cells[1].size), scratch=[pltpu.VMEM((planes, rows, width), jnp.float32)], after=after,
    )


def y_send_kernel(meta, paired, own, other, table, out):
    for plane in range(out.shape[0]):
        out[plane] = along_y(meta, (paired, own, other), plane, table)


def along_y_send(cells, meta, first, after=()):
    planes, rows, width = cells[1].shape
    planes -= first
    return call(
        y_send_kernel, "along_y", meta, y_operands(cells, planes, first), [(planes, rows, width)], y_work(cells[1].size // 2),
        after=after,
    )[0]


def z_kernel(meta, table, *refs):
    count = len(refs) // 2
    ins, outs = refs[:count], refs[count:]
    planes, rows, width = ins[0].shape
    kernel = table[...]
    for tile in range(rows // 8):
        here = pl.ds(8 * tile, 8)
        for begin in range(0, width, BLOCK):
            columns = pl.ds(begin, min(BLOCK, width - begin))
            values = [part[k, here, columns] for part in ins for k in range(planes)]
            highest_value = jnp.maximum(functools.reduce(jnp.maximum, values), LOWEST)
            weights = jnp.concatenate([jnp.exp(value - highest_value) for value in values], axis=0)
            logs = jnp.log(two_term_sum(kernel, weights))
            for o in range(count * planes):
                outs[o // planes][o % planes, here, columns] = logs[8 * o : 8 * o + 8] + highest_value


def z_table(place, slots, depth):
    cell = jnp.arange(slots * depth * 8) // 8
    row = jnp.arange(slots * depth * 8) % 8
    cell = lax.bitwise_xor(cell // depth, place) * depth + cell % depth
    apart = cell[:, None] - cell[None, :]
    distance = apart.astype(jnp.float32)
    values = jnp.exp(-2.0 * distance * distance / float(RADIUS * RADIUS))
    values = jnp.where((jnp.abs(apart) <= RADIUS) & (row[:, None] == row[None, :]), values, 0.0)
    high = lax.reduce_precision(values, 8, 7)
    return jnp.concatenate([high, values - high], axis=0).astype(jnp.bfloat16)


def along_z(parts, table, meta, after=(), weight=1):
    count = len(parts) * parts[0].size
    return call(
        z_kernel, "along_z", meta, [(array, all_of(array)) for array in [table] + parts], [part.shape for part in parts],
        (768 * count * weight, 2 * count), after=after,
    )


def join_kernel(meta, *refs):
    ins, out = refs[:-1], refs[-1]
    for part, (here, columns) in zip(ins, tiles(meta[0], ins, out.shape[1])):
        out[:, here, columns] = part[...]


def join(parts, meta, cuts, first=0, after=(), after_far=False):
    planes, part, width = parts[0].shape
    block = planes - first
    spec = pl.BlockSpec((block, part, width), lambda i, m: (first // block, 0, 0))
    shape = (block, part * len(parts) // cuts, width * cuts)
    return call(
        join_kernel, "join", meta, [(array, spec) for array in parts], [shape], (0, 0), after=after, after_far=after_far
    )[0]


def final_kernel(pieces, meta, *refs):
    refs = list(refs)
    ins = [[refs.pop(0) for _ in range(count + 1)] for count, _, _ in pieces]
    held_in, sems = refs[-1 - len(pieces) : -1], refs[-1]
    outs = refs[-3 - len(pieces) : -1 - len(pieces)]
    depth = ins[0][-1].shape[0]
    half = outs[0].shape[2] // 2
    copies = []
    for at, (count, mine, start) in enumerate(pieces):
        cells, outer, held = ins[at][:-1], ins[at][-1], held_in[at]
        width = outer.shape[2]
        column = pl.multiple_of((meta[3] if mine else 1 - meta[3]) * half + start, width)
        for plane in range(depth):
            if count == 4 and cells[0].shape == outer.shape:
                logs = along_y(meta, cells[:3], plane, cells[3])
                held[0, plane], held[1, plane] = proximal(logs, outer[plane])
            elif count == 1:
                held[0, plane], held[1, plane] = proximal(cells[0][plane], outer[plane])
            else:
                for part, (here, columns) in zip(cells, tiles(meta[0], cells, outer.shape[1])):
                    results = proximal(part[plane], outer[plane, here, columns])
                    held[0, plane, here, columns], held[1, plane, here, columns] = results
            for k, out in enumerate(outs):
                copies.append(
                    pltpu.make_async_copy(
                        held.at[k, plane], out.at[plane, :, pl.ds(column, width)], sems.at[2 * (at * depth + plane) + k]
                    )
                )
                copies[-1].start()
    for copy in copies:
        copy.wait()


def final(pieces, external, meta, before):
    depth, rows, length = external.shape
    operands, kinds, scratch, size = [], [], [], 0
    for given, mine, start, width in pieces:
        place = lambda i, m, mine=mine, start=start, width=width: (0, 0, ((m[3] if mine else 1 - m[3]) * (length // 2) + start) // width)
        operands += given + [(external, pl.BlockSpec((depth, rows, width), place))]
        kinds.append((len(given), mine, start))
        scratch.append(pltpu.VMEM((2, depth, rows, width), jnp.float32))
        size += depth * rows * width
    aliases = {1 + len(operands) + i: i for i in range(len(before))}
    operands += [(array, pl.BlockSpec(memory_space=pltpu.HBM)) for array in before]
    return call(
        functools.partial(final_kernel, kinds), "proximal", meta, operands, [external.shape] * 2, (20 * size, 6 * size),
        aliases, scratch + [pltpu.SemaphoreType.DMA((2 * depth * len(pieces),))], in_place=True,
    )


def own_planes(arrays, depth):
    return [(array, pl.BlockSpec((depth,) + array.shape[1:], lambda i, m: (0, 0, 0))) for array in arrays]


def pairs(count, first):
    ends = [(i, i + 1) for i in range(first, count - 1, 2)]
    return ends + [(j, i) for i, j in ends]


def neighbours(cells):
    count = lax.axis_size("gy")
    return lax.ppermute(cells, "gy", pairs(count, 0)), cells, lax.ppermute(cells, "gy", pairs(count, 1))


def row_meta():
    place, count = lax.axis_index("gy"), lax.axis_size("gy")
    odd = place % 2
    return [place + 1 - odd >= count, (place == 0) | (place + odd >= count), odd]


def swap(cells, bits):
    return lax.ppermute(cells, "gz", [(i, i ^ bits) for i in range(lax.axis_size("gz"))])


def exchange(parts):
    order = sorted(range(1, len(parts)), key=lambda r: -bin(r).count("1"))
    moved = dict((r, swap(parts[r], 2 * r)) for r in order)
    return [parts[0]] + [moved[r] for r in range(1, len(parts))]


def in_parts(potential, external):
    slots = lax.axis_size("gz")
    depth, rows, length = potential.shape
    parts = slots // 2
    place = lax.axis_index("gz")
    first_missing, second_missing, odd = row_meta()
    meta = jnp.stack([place // 2, first_missing, second_missing, place % 2, odd]).astype(jnp.int32)
    table = z_table(place, slots, depth)

    width = length // 4
    later = along_x(potential, meta, False, width, width, 0, far=True)[0]
    first = along_x(potential, meta, False, 0, width, 0, after=[later])[0]
    later = along_x(potential, meta, True, width, width, parts, swap(later, 1))
    first = along_x(potential, meta, True, 0, width, 0, swap(first, 1), after=later)[0]
    own_first = first

    def over_z(cells, cuts):
        cells = [exchange(cells[i * parts : (i + 1) * parts]) for i in range(cuts)]
        return [along_z(part, table, meta) for part in cells]

    def back(cells):
        return [part for parts in cells for part in exchange(parts)]

    first = neighbours(first)
    later = [along_z(exchange(later), table, meta, [own_first], 30)]
    later = join(back(later), meta, LATER_CUTS)
    first = along_y_parts(first, meta, parts, FIRST_CUTS, after=[later])
    later = neighbours(later)
    first = over_z(first, FIRST_CUTS)
    given = swap(along_y_send(later, meta, depth, after=first[-1]), 1)
    first = back(first)
    outs = final([(y_operands(later, depth), True, width, width)], external, meta, [])
    lent = swap(join(first, meta, FIRST_CUTS, depth, after=outs, after_far=True), 1)
    other = (own_planes([given], depth), False, width, width)
    own = (own_planes(first, depth), True, 0, width)
    outs = final([other, own], external, meta, outs)
    return tuple(final([(own_planes([lent], depth), False, 0, width)], external, meta, outs))


def whole(potential, external):
    depth = RADIUS
    slots = lax.axis_size("gz")
    position, devices = lax.axis_index("gy"), lax.axis_size("gy")
    planes, rows, length = potential.shape

    def table(in_index, out_index):
        apart = in_index[:, None] - out_index[None, :]
        distance = apart.astype(jnp.float32)
        values = jnp.exp(-2.0 * distance * distance / float(RADIUS * RADIUS))
        return jnp.where(jnp.abs(apart) <= RADIUS, values, 0.0)

    def summed(equation, window, axis, kernel):
        highest_value = jnp.max(window, axis=axis, keepdims=True)
        weights = jnp.exp(window - highest_value)
        return jnp.log(jnp.einsum(equation, weights, kernel, precision=HIGHEST)) + highest_value

    border = jnp.full((planes, rows, depth), -jnp.inf, jnp.float32)
    padded = jnp.concatenate([border, potential, border], axis=-1)
    pieces = padded.reshape(planes, rows, length // BLOCK + 1, BLOCK)
    window = jnp.concatenate([pieces[..., :-1, :], pieces[..., 1:, :]], axis=-1)
    kernel = table(jnp.arange(2 * BLOCK) - depth, jnp.arange(BLOCK))
    logs = summed("...w,wo->...o", window, -1, kernel).reshape(potential.shape)

    paired, _, other = neighbours(logs)
    up, down = jnp.where(position % 2 == 0, other, paired), jnp.where(position % 2 == 0, paired, other)
    up = jnp.where(position == 0, -jnp.inf, up[:, rows - depth :])
    down = jnp.where(position == devices - 1, -jnp.inf, down[:, :depth])
    window = jnp.concatenate([up, logs, down], axis=1)
    kernel = table(jnp.arange(rows + 2 * depth) - depth, jnp.arange(rows))
    logs = summed("zwx,wo->zox", window, 1, kernel)

    logs = lax.all_to_all(logs, "gz", split_axis=1, concat_axis=0, tiled=True)
    cells = jnp.arange(slots * planes)
    logs = summed("wyx,wo->oyx", logs, 0, table(cells, cells))
    logs = lax.all_to_all(logs, "gz", split_axis=0, concat_axis=1, tiled=True)
    return proximal(logs, external)


def local(potential, external):
    slots = lax.axis_size("gz")
    depth, rows, length = potential.shape
    tiles = slots > 2 and slots & (slots - 1) == 0 and rows % (4 * slots) == 0 and slots * depth <= 32
    if tiles and rows == RADIUS and length % (4 * BLOCK) == 0:
        return in_parts(potential, external)
    return whole(potential, external)


def solution(mesh):
    return jax.shard_map(
        local,
        mesh=mesh,
        in_specs=(P("gz", "gy", None), P("gz", "gy", None)),
        out_specs=(P("gz", "gy", None), P("gz", "gy", None)),
        check_vma=False,
    )
```

```python
import functools

import jax
import jax.numpy as jnp
import ml_dtypes
import numpy as np
from jax import lax
from jax.experimental import pallas as pl
from jax.experimental.pallas import tpu as pltpu
from jax.sharding import PartitionSpec as P

RADIUS = 128
BLOCK = 2 * RADIUS
VMEM_BYTES = 24 * 1024 * 1024
FIRST_CUTS, LATER_CUTS = 1, 1
LOWEST = -1e30

HIGHEST = lax.Precision.HIGHEST


def gauss(apart):
    apart = np.asarray(apart, np.float64)
    table = np.exp(-2.0 * apart * apart / float(RADIUS * RADIUS))
    return np.where(np.abs(apart) <= RADIUS, table, 0.0)


def two_terms(table):
    high = table.astype(ml_dtypes.bfloat16)
    low = (table - high.astype(np.float64)).astype(ml_dtypes.bfloat16)
    return high, low


def x_tables():
    table = gauss(np.arange(2 * BLOCK)[:, None] - RADIUS - np.arange(BLOCK)[None, :])
    return two_terms(table)


def y_table(rows):
    table = gauss(np.arange(rows + 2 * RADIUS)[None, :] - RADIUS - np.arange(rows)[:, None])
    before, own, behind = np.split(table, [RADIUS, RADIUS + rows], axis=1)
    tables = [[before, own, behind], [behind, own, before]]
    return np.concatenate([term for blocks in tables for term in two_terms(np.concatenate(blocks, axis=1))], axis=0)


def split(weights):
    high = weights.astype(jnp.bfloat16)
    low = (weights - high.astype(jnp.float32)).astype(jnp.bfloat16)
    return high, low


def dot(a, b):
    return jnp.dot(a, b, preferred_element_type=jnp.float32)


def x_window(window, high_table, low_table):
    highest_value = jnp.max(window, axis=-1, keepdims=True)
    high, low = split(jnp.exp(window - highest_value))
    summed = dot(high, high_table) + (dot(low, high_table) + dot(high, low_table))
    return jnp.log(summed) + highest_value


def two_term_sum(table, weights):
    rows = table.shape[0] // 2
    high, low = split(weights)
    both = dot(table, high)
    return both[:rows] + (both[rows:] + dot(table[:rows], low))


def y_window(window, table):
    highest_value = jnp.max(window, axis=0, keepdims=True)
    return jnp.log(two_term_sum(table, jnp.exp(window - highest_value))) + highest_value


def proximal(logs, outer_field):
    shifted = logs - 0.5 * outer_field
    level = 1.0 + (jnp.maximum(shifted, 0.0) + jnp.log(1.0 + jnp.exp(-jnp.abs(shifted))))
    log_level = jnp.log(level)
    for newton_step in range(2):
        if newton_step:
            level = jnp.exp(log_level)
        log_level = (level * (log_level - 1.0) + shifted) / (1.0 + level)
    return log_level - logs, log_level


def slot_rows(place, slot, rows):
    return pl.ds(pl.multiple_of(lax.bitwise_xor(place, slot) * rows, rows), rows)


def tiles(place, parts, rows):
    part, width = parts[0].shape[1:]
    count = rows // part
    return [(slot_rows(place, at % count, part), pl.ds(at // count * width, width)) for at in range(len(parts))]


def all_of(array):
    return pl.BlockSpec(array.shape, lambda i, m: (0,) * array.ndim)


def call(kernel, name, meta, operands, outs, work, aliases={}, scratch=(), after=(), after_far=False, in_place=False):
    used = 1 + len(operands)
    if after_far:
        after = [pltpu.with_memory_space_constraint(array, pltpu.HBM) for array in after]
    operands = operands + [(array, pl.BlockSpec(memory_space=pl.ANY)) for array in after]

    def body(*refs):
        kernel(*refs[:used], *refs[used + len(after) :])

    shapes = [jax.ShapeDtypeStruct(shape, jnp.float32) for shape in outs]
    return pl.pallas_call(
        body,
        grid_spec=pltpu.PrefetchScalarGridSpec(
            num_scalar_prefetch=1,
            grid=(1,),
            in_specs=[spec for _, spec in operands],
            out_specs=[pl.BlockSpec(memory_space=pltpu.HBM) if in_place else all_of(shape) for shape in shapes],
            scratch_shapes=list(scratch),
        ),
        out_shape=shapes,
        input_output_aliases=aliases,
        compiler_params=pltpu.CompilerParams(vmem_limit_bytes=VMEM_BYTES),
        cost_estimate=pl.CostEstimate(
            flops=2 * work[0], bytes_accessed=8 * sum(int(np.prod(shape)) for shape in outs), transcendentals=work[1]
        ),
        name=name,
    )(meta, *[array for array, _ in operands])


def x_kernel(edges, received, parts, meta, main, left, right, high_ref, low_ref, *refs):
    refs = list(refs)
    other = refs.pop(0) if received else None
    held = refs.pop() if parts else None
    depth, rows, width = main.shape
    own = slice(0, depth)

    def ended(edge, which):
        return jnp.where(meta[3] == which - 1, -jnp.inf, edge) if which else edge

    cells = [ended(left[...], edges[0]), main[...], ended(right[...], edges[1])]
    cells = jnp.concatenate([piece.reshape(depth * rows, piece.shape[-1]) for piece in cells], axis=-1)
    for j in range(width // BLOCK):
        window = cells[:, j * BLOCK : (j + 2) * BLOCK]
        result = x_window(window, high_ref[...], low_ref[...]).reshape(depth, rows, BLOCK)
        columns = pl.ds(j * BLOCK, BLOCK)
        if parts:
            held[:, :, columns] = result
        else:
            refs[0][own, :, columns] = result
    if parts:
        for out, (here, columns) in zip(refs, tiles(meta[0], refs, rows)):
            out[own] = held[:, here, columns]
            out[depth:] = other[:, here, columns]
    elif received:
        refs[0][depth:] = other[...]


def along_x(potential, meta, mine, start, width, parts, received=None, cuts=1, after=(), far=False):
    depth, rows, length = potential.shape
    half = length // 2

    def begin(m, unit):
        return (m[3] if mine else 1 - m[3]) * (half // unit) + start // unit

    edges = (0 if start else (1 if mine else 2)), (0 if start + width < half else (2 if mine else 1))
    before = lambda i, m: (0, 0, jnp.maximum(begin(m, RADIUS) - 1, 0))
    behind = lambda i, m: (0, 0, jnp.minimum(begin(m, RADIUS) + width // RADIUS, length // RADIUS - 1))
    operands = [
        (potential, pl.BlockSpec((depth, rows, width), lambda i, m: (0, 0, begin(m, width)))),
        (potential, pl.BlockSpec((depth, rows, RADIUS), before)),
        (potential, pl.BlockSpec((depth, rows, RADIUS), behind)),
    ]
    operands += [(jnp.asarray(table), all_of(table)) for table in x_tables()]
    if far:
        operands = [(pltpu.with_memory_space_constraint(array, pltpu.HBM), spec) for array, spec in operands]
    planes = depth
    if received is not None:
        planes = 2 * depth
        operands.append((received, all_of(received)))
    outs = [(planes, rows // parts, width // cuts)] * (parts * cuts) if parts else [(planes, rows, width)]
    count = depth * rows * width
    return call(
        functools.partial(x_kernel, edges, received is not None, parts),
        "along_x", meta, operands, outs, (6 * BLOCK * count, 3 * count),
        scratch=[pltpu.VMEM((depth, rows, width), jnp.float32)] if parts else [], after=after,
    )


def along_y(meta, cells, plane, table):
    other, own, paired = cells
    cells = [
        jnp.where(meta[2] == 1, -jnp.inf, other[plane]),
        own[plane],
        jnp.where(meta[1] == 1, -jnp.inf, paired[plane]),
    ]
    return y_window(jnp.concatenate(cells, axis=0), table[...])


def y_operands(cells, planes, first=0):
    rows, width = cells[1].shape[1:]
    operands = [(array, pl.BlockSpec((planes, rows, width), lambda i, m: (first // planes, 0, 0))) for array in cells]
    table = y_table(rows)
    return operands + [(jnp.asarray(table), pl.BlockSpec((2 * rows, table.shape[1]), lambda i, m: (m[4], 0)))]


def y_work(count):
    return 12 * RADIUS * count, 4 * count


def y_parts_kernel(meta, other, own, paired, table, *refs):
    outs, held = refs[:-1], refs[-1]
    planes, rows, width = own.shape
    for plane in range(planes):
        held[plane] = along_y(meta, (other, own, paired), plane, table)
    for out, (here, columns) in zip(outs, tiles(meta[0], outs, rows)):
        out[...] = held[:, here, columns]


def along_y_parts(cells, meta, parts, cuts=1, after=()):
    planes, rows, width = cells[1].shape
    return call(
        y_parts_kernel, "along_y", meta, y_operands(cells, planes), [(planes, rows // parts, width // cuts)] * (parts * cuts),
        y_work(cells[1].size), scratch=[pltpu.VMEM((planes, rows, width), jnp.float32)], after=after,
    )


def y_send_kernel(meta, other, own, paired, table, out):
    for plane in range(out.shape[0]):
        out[plane] = along_y(meta, (other, own, paired), plane, table)


def along_y_send(cells, meta, first, after=()):
    planes, rows, width = cells[1].shape
    planes -= first
    return call(
        y_send_kernel, "along_y", meta, y_operands(cells, planes, first), [(planes, rows, width)], y_work(cells[1].size // 2),
        after=after,
    )[0]


def z_kernel(meta, table, *refs):
    count = len(refs) // 2
    ins, outs = refs[:count], refs[count:]
    planes, rows, width = ins[0].shape
    kernel = table[...]
    for tile in range(rows // 8):
        here = pl.ds(8 * tile, 8)
        for begin in range(0, width, BLOCK):
            columns = pl.ds(begin, min(BLOCK, width - begin))
            values = [part[k, here, columns] for part in ins for k in range(planes)]
            highest_value = jnp.maximum(functools.reduce(jnp.maximum, values), LOWEST)
            weights = jnp.concatenate([jnp.exp(value - highest_value) for value in values], axis=0)
            logs = jnp.log(two_term_sum(kernel, weights))
            for o in range(count * planes):
                outs[o // planes][o % planes, here, columns] = logs[8 * o : 8 * o + 8] + highest_value


def z_table(place, slots, depth):
    cell = jnp.arange(slots * depth * 8) // 8
    row = jnp.arange(slots * depth * 8) % 8
    cell = lax.bitwise_xor(cell // depth, place) * depth + cell % depth
    apart = cell[:, None] - cell[None, :]
    distance = apart.astype(jnp.float32)
    values = jnp.exp(-2.0 * distance * distance / float(RADIUS * RADIUS))
    values = jnp.where((jnp.abs(apart) <= RADIUS) & (row[:, None] == row[None, :]), values, 0.0)
    high = lax.reduce_precision(values, 8, 7)
    return jnp.concatenate([high, values - high], axis=0).astype(jnp.bfloat16)


def along_z(parts, table, meta, after=(), weight=1):
    count = len(parts) * parts[0].size
    return call(
        z_kernel, "along_z", meta, [(array, all_of(array)) for array in [table] + parts], [part.shape for part in parts],
        (768 * count * weight, 2 * count), after=after,
    )


def join_kernel(meta, *refs):
    ins, out = refs[:-1], refs[-1]
    for part, (here, columns) in zip(ins, tiles(meta[0], ins, out.shape[1])):
        out[:, here, columns] = part[...]


def join(parts, meta, cuts, first=0, after=(), after_far=False):
    planes, part, width = parts[0].shape
    block = planes - first
    spec = pl.BlockSpec((block, part, width), lambda i, m: (first // block, 0, 0))
    shape = (block, part * len(parts) // cuts, width * cuts)
    return call(
        join_kernel, "join", meta, [(array, spec) for array in parts], [shape], (0, 0), after=after, after_far=after_far
    )[0]


def final_kernel(pieces, meta, *refs):
    refs = list(refs)
    ins = [[refs.pop(0) for _ in range(count + 1)] for count, _, _ in pieces]
    held_in, sems = refs[-1 - len(pieces) : -1], refs[-1]
    outs = refs[-3 - len(pieces) : -1 - len(pieces)]
    depth = ins[0][-1].shape[0]
    half = outs[0].shape[2] // 2
    copies = []
    for at, (count, mine, start) in enumerate(pieces):
        cells, outer, held = ins[at][:-1], ins[at][-1], held_in[at]
        width = outer.shape[2]
        column = pl.multiple_of((meta[3] if mine else 1 - meta[3]) * half + start, width)
        for plane in range(depth):
            if count == 4 and cells[0].shape == outer.shape:
                logs = along_y(meta, cells[:3], plane, cells[3])
                held[0, plane], held[1, plane] = proximal(logs, outer[plane])
            elif count == 1:
                held[0, plane], held[1, plane] = proximal(cells[0][plane], outer[plane])
            else:
                for part, (here, columns) in zip(cells, tiles(meta[0], cells, outer.shape[1])):
                    results = proximal(part[plane], outer[plane, here, columns])
                    held[0, plane, here, columns], held[1, plane, here, columns] = results
            for k, out in enumerate(outs):
                copies.append(
                    pltpu.make_async_copy(
                        held.at[k, plane], out.at[plane, :, pl.ds(column, width)], sems.at[2 * (at * depth + plane) + k]
                    )
                )
                copies[-1].start()
    for copy in copies:
        copy.wait()


def final(pieces, external, meta, before):
    depth, rows, length = external.shape
    operands, kinds, scratch, size = [], [], [], 0
    for given, mine, start, width in pieces:
        place = lambda i, m, mine=mine, start=start, width=width: (0, 0, ((m[3] if mine else 1 - m[3]) * (length // 2) + start) // width)
        operands += given + [(external, pl.BlockSpec((depth, rows, width), place))]
        kinds.append((len(given), mine, start))
        scratch.append(pltpu.VMEM((2, depth, rows, width), jnp.float32))
        size += depth * rows * width
    aliases = {1 + len(operands) + i: i for i in range(len(before))}
    operands += [(array, pl.BlockSpec(memory_space=pltpu.HBM)) for array in before]
    return call(
        functools.partial(final_kernel, kinds), "proximal", meta, operands, [external.shape] * 2, (20 * size, 6 * size),
        aliases, scratch + [pltpu.SemaphoreType.DMA((2 * depth * len(pieces),))], in_place=True,
    )


def own_planes(arrays, depth):
    return [(array, pl.BlockSpec((depth,) + array.shape[1:], lambda i, m: (0, 0, 0))) for array in arrays]


def pairs(count, first):
    ends = [(i, i + 1) for i in range(first, count - 1, 2)]
    return ends + [(j, i) for i, j in ends]


def neighbours(cells):
    count = lax.axis_size("gy")
    paired = lax.ppermute(cells, "gy", pairs(count, 0))
    return lax.ppermute(cells, "gy", pairs(count, 1)), cells, paired


def row_meta():
    place, count = lax.axis_index("gy"), lax.axis_size("gy")
    odd = place % 2
    return [place + 1 - odd >= count, (place == 0) | (place + odd >= count), odd]


def swap(cells, bits):
    return lax.ppermute(cells, "gz", [(i, i ^ bits) for i in range(lax.axis_size("gz"))])


def exchange(parts):
    order = sorted(range(1, len(parts)), key=lambda r: -bin(r).count("1"))
    moved = dict((r, swap(parts[r], 2 * r)) for r in order)
    return [parts[0]] + [moved[r] for r in range(1, len(parts))]


def in_parts(potential, external):
    slots = lax.axis_size("gz")
    depth, rows, length = potential.shape
    parts = slots // 2
    place = lax.axis_index("gz")
    first_missing, second_missing, odd = row_meta()
    meta = jnp.stack([place // 2, first_missing, second_missing, place % 2, odd]).astype(jnp.int32)
    table = z_table(place, slots, depth)

    width = length // 4
    later = along_x(potential, meta, False, width, width, 0, far=True)[0]
    first = along_x(potential, meta, False, 0, width, 0, after=[later])[0]
    later = along_x(potential, meta, True, width, width, parts, swap(later, 1))
    first = along_x(potential, meta, True, 0, width, 0, swap(first, 1), after=later)[0]
    own_first = first

    def over_z(cells, cuts):
        cells = [exchange(cells[i * parts : (i + 1) * parts]) for i in range(cuts)]
        return [along_z(part, table, meta) for part in cells]

    def back(cells):
        return [part for parts in cells for part in exchange(parts)]

    first = neighbours(first)
    later = [along_z(exchange(later), table, meta, [own_first], 30)]
    later = join(back(later), meta, LATER_CUTS)
    first = along_y_parts(first, meta, parts, FIRST_CUTS, after=[later])
    later = neighbours(later)
    first = over_z(first, FIRST_CUTS)
    given = swap(along_y_send(later, meta, depth, after=first[-1]), 1)
    first = back(first)
    outs = final([(y_operands(later, depth), True, width, width)], external, meta, [])
    lent = swap(join(first, meta, FIRST_CUTS, depth, after=outs, after_far=True), 1)
    other = (own_planes([given], depth), False, width, width)
    own = (own_planes(first, depth), True, 0, width)
    outs = final([other, own], external, meta, outs)
    return tuple(final([(own_planes([lent], depth), False, 0, width)], external, meta, outs))


def whole(potential, external):
    depth = RADIUS
    slots = lax.axis_size("gz")
    position, devices = lax.axis_index("gy"), lax.axis_size("gy")
    planes, rows, length = potential.shape

    def table(in_index, out_index):
        apart = in_index[:, None] - out_index[None, :]
        distance = apart.astype(jnp.float32)
        values = jnp.exp(-2.0 * distance * distance / float(RADIUS * RADIUS))
        return jnp.where(jnp.abs(apart) <= RADIUS, values, 0.0)

    def summed(equation, window, axis, kernel):
        highest_value = jnp.max(window, axis=axis, keepdims=True)
        weights = jnp.exp(window - highest_value)
        return jnp.log(jnp.einsum(equation, weights, kernel, precision=HIGHEST)) + highest_value

    border = jnp.full((planes, rows, depth), -jnp.inf, jnp.float32)
    padded = jnp.concatenate([border, potential, border], axis=-1)
    pieces = padded.reshape(planes, rows, length // BLOCK + 1, BLOCK)
    window = jnp.concatenate([pieces[..., :-1, :], pieces[..., 1:, :]], axis=-1)
    kernel = table(jnp.arange(2 * BLOCK) - depth, jnp.arange(BLOCK))
    logs = summed("...w,wo->...o", window, -1, kernel).reshape(potential.shape)

    other, _, paired = neighbours(logs)
    up, down = jnp.where(position % 2 == 0, other, paired), jnp.where(position % 2 == 0, paired, other)
    up = jnp.where(position == 0, -jnp.inf, up[:, rows - depth :])
    down = jnp.where(position == devices - 1, -jnp.inf, down[:, :depth])
    window = jnp.concatenate([up, logs, down], axis=1)
    kernel = table(jnp.arange(rows + 2 * depth) - depth, jnp.arange(rows))
    logs = summed("zwx,wo->zox", window, 1, kernel)

    logs = lax.all_to_all(logs, "gz", split_axis=1, concat_axis=0, tiled=True)
    cells = jnp.arange(slots * planes)
    logs = summed("wyx,wo->oyx", logs, 0, table(cells, cells))
    logs = lax.all_to_all(logs, "gz", split_axis=0, concat_axis=1, tiled=True)
    return proximal(logs, external)


def local(potential, external):
    slots = lax.axis_size("gz")
    depth, rows, length = potential.shape
    tiles = slots > 2 and slots & (slots - 1) == 0 and rows % (4 * slots) == 0 and slots * depth <= 32
    if tiles and rows == RADIUS and length % (4 * BLOCK) == 0:
        return in_parts(potential, external)
    return whole(potential, external)


def solution(mesh):
    return jax.shard_map(
        local,
        mesh=mesh,
        in_specs=(P("gz", "gy", None), P("gz", "gy", None)),
        out_specs=(P("gz", "gy", None), P("gz", "gy", None)),
        check_vma=False,
    )
```
